32 devices in a mesh: group: 2 (over y), shard: 16 (over z, x, core).
Axes of the slice: x: 2, y: 2, z: 4, core: 2. Of those that a mesh axis runs over, the one named last changes fastest.
Arguments:
- gradients: bfloat16 [2, 16, 256, 8192], P('group', 'shard'), may hold values from -1.59375 to 1.59375
- momentum: float32 [2, 256, 8192], P('group', None, 'shard'), may hold values from -6 to 6
- master: float32 [256, 8192], P(None, 'shard'), may hold values from -0.6 to 0.6
- indices: int32 [2, 4, 128, 32], P('group', None, 'shard'), may hold values from 0 to 4095, as said below
Outputs:
- momentum_out: float32 [2, 256, 8192], P('group', None, 'shard')
- master_out: float32 [256, 8192], P(None, 'shard')
- params_full: bfloat16 [256, 8192], replicated
The draws below stay inside these ranges and needn't reach their ends.
Inputs may be any that keep to these rules, and one draw needn't show every extreme that they name: `indices`: the 32 positions of one group and block are distinct.
All inputs are finite; a program needn't handle non-finite values.
Results may differ from the reference program's by a relative error of at most 0.001.
Values may be sent and summed in bfloat16 or wider, within the bound.
A program may use at most 128 MiB of HBM per device.

```python
import jax
import jax.numpy as jnp
from jax import lax

D = 8192
ROWS = 256
BLOCK = 64
TOPK = 32
N_GROUP = 2
N_SHARD = 16


def draw_indices(key, part):
    scores = jax.random.randint(key, (N_GROUP, ROWS // BLOCK, D // BLOCK, BLOCK * BLOCK), 0, 2 ** 18)
    scores = scores * (BLOCK * BLOCK) + lax.broadcasted_iota(jnp.int32, scores.shape, 3)
    return lax.top_k(scores, TOPK)[1].astype(jnp.int32)


def strengthened(entries, stream_key, source, target, blocks, factor):
    def block_of(position):
        return (jnp.arange(entries.shape[position]) // (entries.shape[position] // blocks)).reshape((-1,) + (1,) * (entries.ndim - 1 - position))

    near = jax.random.permutation(stream_key, blocks)[block_of(target)]
    far = (block_of(target) + blocks // 2) % blocks
    return jnp.where((block_of(source) == near) | (block_of(source) == far), factor * entries, entries)


def levels(rng, dims, split, smallest, top_value):
    def one(position, blocks):
        draws = jax.random.uniform(jax.random.fold_in(jax.random.fold_in(rng, 6), position), (blocks,), jnp.float32, smallest / len(split), top_value / len(split))
        return jnp.repeat(jnp.exp(draws), dims[position] // blocks).reshape((-1,) + (1,) * (len(dims) - position - 1))

    level = one(*split[0])
    for cut in split[1:]:
        level = level * one(*cut)
    return level


def bell_draw(own_key, shape, deviation, bound, shards=(), kind=jnp.bfloat16):
    values = deviation * jax.random.normal(own_key, shape, jnp.float32)
    if shards:
        values = values * levels(own_key, shape, shards, -0.22, 0.18)
    return jnp.clip(values, -bound, bound).astype(kind)


def heavy_noise(key, dims, width, most, shards, heavy, kind=jnp.bfloat16):
    entries = width * jax.random.normal(key, dims, jnp.float32)
    if shards:
        entries = entries * levels(key, dims, shards, -0.22, 0.18)
    return jnp.clip(strengthened(entries, jax.random.fold_in(key, 3), *heavy), -most, most).astype(kind)


def setup_inputs(seed: int = 0) -> dict:
    keys = jax.random.split(jax.random.key(seed), 5)
    return {
        "gradients": heavy_noise(keys[0], (N_GROUP, N_SHARD, ROWS, D), 0.2, 1.59375, ((0, 2), (1, 16)), (1, 3, 16, 2.0)),
        "momentum": bell_draw(keys[1], (N_GROUP, ROWS, D), 1.0, 6.0, ((0, 2), (2, 16)), jnp.float32),
        "master": bell_draw(keys[2], (ROWS, D), 0.1, 0.6, ((1, 16),), jnp.float32),
        "indices": draw_indices(jax.random.fold_in(keys[4], 71), 0),
    }


momentum_decay = 0.9
step_rate = 0.5

def cosine_table(side):
    freqs = jnp.arange(side, dtype=jnp.float32)[:, None]
    places = jnp.arange(side, dtype=jnp.float32)[None, :]
    table = jnp.cos(jnp.pi * (2.0 * places + 1.0) * freqs / (2.0 * side))
    weights = jnp.where(freqs == 0.0, jnp.sqrt(1.0 / side), jnp.sqrt(2.0 / side))
    return table * weights

def into_blocks(field, side):
    leading = field.shape[:-2]
    depth = len(leading)
    shaped = field.reshape(leading + (field.shape[-2] // side, side, field.shape[-1] // side, side))
    return jnp.moveaxis(shaped, depth + 2, depth + 1)

def out_blocks(blocks):
    leading = blocks.shape[:-4]
    depth = len(leading)
    moved = jnp.moveaxis(blocks, depth + 1, depth + 2)
    return moved.reshape(leading + (blocks.shape[-4] * blocks.shape[-2], blocks.shape[-3] * blocks.shape[-1]))

def forward_blocks(blocks, table):
    return jnp.einsum('kn,...nm,lm->...kl', table, blocks, table, precision=lax.Precision.HIGHEST)

def inverse_blocks(blocks, table):
    return jnp.einsum('kn,...kl,lm->...nm', table, blocks, table, precision=lax.Precision.HIGHEST)

def scatter_picked(picked, positions, target_shape):
    places = [lax.broadcasted_iota(jnp.int32, positions.shape, dimension) for dimension in range(positions.ndim - 1)]
    return jnp.zeros(target_shape, picked.dtype).at[tuple(places) + (positions,)].add(picked)

def reference(gradients, momentum, master, indices):
    table = cosine_table(BLOCK)

    def add_device(device_index, running):
        piece = lax.dynamic_index_in_dim(gradients, device_index, 1, keepdims=False)
        return running + piece.astype(jnp.float32)
    summed = lax.fori_loop(0, N_SHARD, add_device, jnp.zeros((N_GROUP, ROWS, D), jnp.float32))
    accumulated = momentum_decay * momentum + summed
    coeffs = forward_blocks(into_blocks(accumulated, BLOCK), table)
    flat = coeffs.reshape(coeffs.shape[:-2] + (BLOCK * BLOCK,))
    picked = jnp.take_along_axis(flat, indices, axis=3)
    own_dense = scatter_picked(picked, indices, flat.shape)
    union_sum = lax.optimization_barrier(jnp.sum(own_dense, axis=0))
    own_field = out_blocks(inverse_blocks(own_dense.reshape(coeffs.shape), table))
    momentum_out = accumulated - own_field
    change_field = out_blocks(inverse_blocks(union_sum.reshape(coeffs.shape[1:]), table))
    master_out = master - step_rate * jnp.tanh(change_field)
    return (momentum_out, master_out, master_out.astype(jnp.bfloat16))
```

```python
import functools

import jax
import jax.numpy as jnp
import numpy as np
from jax import lax
from jax.experimental import pallas as pl
from jax.experimental.pallas import tpu as pltpu
from jax.sharding import PartitionSpec as P

BLOCK = 64
LANES = 128
TOP = 32767.0

momentum_decay = 0.9
step_rate = 0.5

HI = lax.Precision.HIGHEST
MESH = pl.DeviceIdType.MESH
F32 = jnp.float32
BF16 = jnp.bfloat16


def cosine_table(side):
    freqs = np.arange(side, dtype=np.float64)[:, None]
    places = np.arange(side, dtype=np.float64)[None, :]
    table = np.cos(np.pi * (2.0 * places + 1.0) * freqs / (2.0 * side))
    weights = np.where(freqs == 0.0, np.sqrt(1.0 / side), np.sqrt(2.0 / side))
    return table * weights


def split3(x):
    high = x.astype(BF16)
    rest = x - high.astype(F32)
    mid = rest.astype(BF16)
    low = (rest - mid.astype(F32)).astype(BF16)
    return high, mid, low


def dot(a, b):
    return jnp.dot(a, b, precision=HI, preferred_element_type=F32)


def dot_nt(a, b, precision=None):
    return lax.dot_general(a, b, (((1,), (1,)), ((), ())), precision=precision, preferred_element_type=F32)


def kernel(n_group, n, width, side,
           grad, mom, master, idx, rt, rtt, ct,
           mom_out, master_out, params_out,
           mine, sib, sendq, recvq, sends, recvs, acc, coefs_t, dense, union, param, idx_all, pick_all,
           mine_sem, raw_send, raw_recv, q_send, q_recv, s_send, s_recv,
           idx_send, idx_recv, pick_send, pick_recv,
           own_sem, ag_send, ag_recv, fw_send, fw_recv):
    rows = master.shape[0]
    half = rows // 2
    height = rows // BLOCK
    steps = n // 2
    count = 2 * steps - 1
    slots = idx.shape[1]
    per_block = slots // (width // BLOCK)

    g = lax.axis_index("group")
    s = lax.axis_index("shard")
    core = lax.rem(s, 2)
    chip = s // 2
    odd = lax.rem(chip, 2)
    pos = (1 - odd) * (chip // 2) + odd * (n - 1 - chip // 2)

    def chip_at(offset):
        place = lax.rem(pos + (offset % n), n)
        back = place // (n // 2)
        return (1 - back) * (2 * place) + back * (2 * (n - 1 - place) + 1)

    sibling = 2 * chip + (1 - core)
    beside = {1: 2 * chip_at(1) + core, -1: 2 * chip_at(-1) + core}

    def columns(shard):
        return pl.ds(pl.multiple_of(shard * width, LANES), width)

    def other_group(k):
        return lax.rem(g + k, n_group)

    barrier = pltpu.get_barrier_semaphore()
    for sign in (1, -1):
        pl.semaphore_signal(barrier, inc=1, device_id={"shard": beside[sign]}, device_id_type=MESH)
    pl.semaphore_signal(barrier, inc=1, device_id={"shard": sibling}, device_id_type=MESH)
    for k in range(1, n_group):
        pl.semaphore_signal(barrier, inc=1, device_id={"group": other_group(k)}, device_id_type=MESH)

    order = [steps]
    for t in range(1, steps):
        order += [steps - t, n - (steps - t)]
    order += [0]

    own_loads = {}
    for r in order:
        own_loads[r] = pltpu.make_async_copy(
            grad.at[0, 0, :, columns(2 * chip_at(r) + core)], mine.at[r], mine_sem.at[r])
        own_loads[r].start()

    pl.semaphore_wait(barrier, 3 + n_group - 1)

    raw = {}
    for r in order:
        raw[r] = pltpu.make_async_remote_copy(
            src_ref=grad.at[0, 0, :, columns(2 * chip_at(r) + 1 - core)], dst_ref=sib.at[r],
            send_sem=raw_send.at[r], recv_sem=raw_recv.at[r],
            device_id={"shard": sibling}, device_id_type=MESH)
        raw[r].start()

    idx_copies = []
    for k in range(1, n_group):
        copy = pltpu.make_async_remote_copy(
            src_ref=idx, dst_ref=idx_all.at[k - 1],
            send_sem=idx_send.at[k - 1], recv_sem=idx_recv.at[k - 1],
            device_id={"group": other_group(k)}, device_id_type=MESH)
        copy.start()
        idx_copies.append(copy)

    def own_first(sign):
        return 0 if sign == 1 else 1

    ready = set()

    def arrived(r):
        if r not in ready:
            ready.add(r)
            own_loads[r].wait()
            raw[r].wait_recv()

    def q_copies(sign, m):
        d = 0 if sign == 1 else 1
        there = {"shard": beside[sign]}
        return (
            pltpu.make_async_remote_copy(
                src_ref=sendq.at[d, m], dst_ref=recvq.at[d, m],
                send_sem=q_send.at[d, m], recv_sem=q_recv.at[d, m],
                device_id=there, device_id_type=MESH),
            pltpu.make_async_remote_copy(
                src_ref=sends.at[d, m], dst_ref=recvs.at[d, m],
                send_sem=s_send.at[d, m], recv_sem=s_recv.at[d, m],
                device_id=there, device_id_type=MESH))

    def message(t, first):
        return 0 if t == 0 else 2 * t - 1 + (1 if first else 0)

    def received(d, m, lane):
        scale = recvs[d, m, 0:1, :]
        return recvq[d, m, :, pl.ds(lane * LANES, LANES)].astype(jnp.int32).astype(F32) * scale

    tiles = width // LANES
    for t in range(steps):
        for first in ((True,) if t == 0 else (False, True)):
            for sign in (1, -1):
                d = 0 if sign == 1 else 1
                part = own_first(sign) if first else 1 - own_first(sign)
                r = (sign * (steps - t)) % n
                m = message(t, first)
                arrived(r)
                has = t >= 2 or (t == 1 and first)
                if has:
                    before = message(t - 1, first)
                    for copy in q_copies(sign, before):
                        copy.wait_recv()
                band = pl.ds(part * half, half)
                values = []
                top = None
                for lane in range(tiles):
                    cols = pl.ds(lane * LANES, LANES)
                    x = mine[r, band, cols].astype(F32) + sib[r, band, cols].astype(F32)
                    if has:
                        x = x + received(d, before, lane)
                    values.append(x)
                    peak = jnp.max(jnp.abs(x), axis=0, keepdims=True)
                    top = peak if top is None else jnp.maximum(top, peak)
                top = jnp.maximum(top, 1e-30)
                inverse = TOP / top
                for lane in range(tiles):
                    q = jnp.round(values[lane] * inverse).astype(jnp.int32).astype(jnp.int16)
                    sendq[d, m, :, pl.ds(lane * LANES, LANES)] = q
                sends[d, m] = jnp.broadcast_to(top * (1.0 / TOP), (8, LANES))
                for copy in q_copies(sign, m):
                    copy.start()

    arrived(0)
    for first in (False, True):
        for sign in (1, -1):
            for copy in q_copies(sign, message(steps - 1, first)):
                copy.wait_recv()
    for part in range(2):
        band = pl.ds(part * half, half)
        for lane in range(tiles):
            cols = pl.ds(lane * LANES, LANES)
            x = mine[0, band, cols].astype(F32) + sib[0, band, cols].astype(F32)
            for sign in (1, -1):
                x = x + received(0 if sign == 1 else 1, message(steps - 1, part == own_first(sign)), lane)
            acc[band, cols] = momentum_decay * mom[0, band, cols] + x

    span = ct.shape[0]
    stage = dot(rt[...], acc[...])
    for tile in range(width // span):
        coefs_t[pl.ds(tile * span, span), :] = dot_nt(ct[...], stage[:, tile * span:(tile + 1) * span], HI)

    lane_block = lax.broadcasted_iota(jnp.int32, (1, slots), 1) // per_block

    def row_hot(ids):
        return lax.broadcasted_iota(jnp.int32, (BLOCK, slots), 0) == (ids >> 6)

    def col_hot(ids):
        places = lane_block * BLOCK + (ids & (BLOCK - 1))
        return lax.broadcasted_iota(jnp.int32, (width, slots), 0) == places

    def spread(ids, picked):
        hot = jnp.where(row_hot(ids), picked, 0.0)
        cols = jnp.where(col_hot(ids), 1.0, 0.0).astype(BF16)
        high, mid, low = split3(hot)
        return dot_nt(high, cols) + (dot_nt(mid, cols) + dot_nt(low, cols))

    high, mid, low = split3(coefs_t[...])
    pick_all[0] = jnp.zeros(pick_all.shape[1:], F32)
    for a in range(height):
        ids = idx[a:a + 1, :]
        hot = lax.broadcasted_iota(jnp.int32, (rows, slots), 0) == (ids >> 6) + a * BLOCK
        hot = jnp.where(hot, 1.0, 0.0).astype(BF16)
        at_row = (jnp.dot(high, hot, preferred_element_type=F32)
                  + (jnp.dot(mid, hot, preferred_element_type=F32)
                     + jnp.dot(low, hot, preferred_element_type=F32)))
        pick_all[0, a:a + 1, :] = jnp.sum(jnp.where(col_hot(ids), at_row, 0.0), axis=0, keepdims=True)

    pick_copies = []
    for k in range(1, n_group):
        copy = pltpu.make_async_remote_copy(
            src_ref=pick_all.at[0], dst_ref=pick_all.at[k],
            send_sem=pick_send.at[k - 1], recv_sem=pick_recv.at[k - 1],
            device_id={"group": other_group(k)}, device_id_type=MESH)
        copy.start()
        pick_copies.append(copy)

    for a in range(height):
        dense[pl.ds(a * BLOCK, BLOCK), :] = spread(idx[a:a + 1, :], pick_all[0, a:a + 1, :])
    union[...] = dense[...]
    for k in range(1, n_group):
        idx_copies[k - 1].wait_recv()
        pick_copies[k - 1].wait_recv()
        for a in range(height):
            band = pl.ds(a * BLOCK, BLOCK)
            union[band, :] = union[band, :] + spread(idx_all[k - 1, a:a + 1, :], pick_all[k, a:a + 1, :])

    def back(field, tile):
        return dot(field[:, tile * span:(tile + 1) * span], ct[...])

    stage = dot(rtt[...], union[...])
    for tile in range(width // span):
        cols = pl.ds(tile * span, span)
        new = master[:, cols] - step_rate * jnp.tanh(back(stage, tile))
        master_out[:, cols] = new
        param[:, cols] = new.astype(BF16)

    def place(offset):
        return columns(2 * chip_at(offset) + core)

    def ag_copy(sign, t, part, m):
        d = 0 if sign == 1 else 1
        band = pl.ds(part * half, half)
        where = params_out.at[band, place(-sign * t)]
        return pltpu.make_async_remote_copy(
            src_ref=param.at[band, :] if t == 0 else where, dst_ref=where,
            send_sem=ag_send.at[d, m], recv_sem=ag_recv.at[d, m],
            device_id={"shard": beside[sign]}, device_id_type=MESH)

    def ag_arrival(sign, t, part, m):
        d = 0 if sign == 1 else 1
        where = params_out.at[pl.ds(part * half, half), place(-sign * (t + 1))]
        return pltpu.make_async_remote_copy(
            src_ref=where, dst_ref=where,
            send_sem=ag_send.at[d, m], recv_sem=ag_recv.at[d, m],
            device_id={"shard": beside[sign]}, device_id_type=MESH)

    def fw_copy(sign, t, part, m, c):
        d = 0 if sign == 1 else 1
        where = params_out.at[pl.ds(part * half, half), columns(2 * chip_at(-sign * (t + 1)) + c)]
        return pltpu.make_async_remote_copy(
            src_ref=where, dst_ref=where,
            send_sem=fw_send.at[d, m], recv_sem=fw_recv.at[d, m],
            device_id={"shard": sibling}, device_id_type=MESH)

    trips = [(t, first) for t in range(steps) for first in ((True, False) if t < steps - 1 else (True,))]
    number = {trip: m for m, trip in enumerate(trips)}

    def part_of(sign, first):
        return own_first(sign) if first else 1 - own_first(sign)

    sent = []

    def go(sign, t, first):
        if (t, first) in number:
            copy = ag_copy(sign, t, part_of(sign, first), number[(t, first)])
            copy.start()
            sent.append(copy)

    for first in (True, False):
        for sign in (1, -1):
            go(sign, 0, first)
    own = pltpu.make_async_copy(param, params_out.at[:, place(0)], own_sem)
    own.start()

    def own_forward(c):
        return pltpu.make_async_remote_copy(
            src_ref=param, dst_ref=params_out.at[:, columns(2 * chip + c)],
            send_sem=fw_send.at[0, count], recv_sem=fw_recv.at[0, count],
            device_id={"shard": sibling}, device_id_type=MESH)

    own_forward(core).start()

    stage = dot(rtt[...], dense[...])
    for tile in range(width // span):
        cols = pl.ds(tile * span, span)
        mom_out[0, :, cols] = acc[:, cols] - back(stage, tile)

    for m, (t, first) in enumerate(trips):
        for sign in (1, -1):
            ag_arrival(sign, t, part_of(sign, first), m).wait_recv()
            go(sign, t + 1, first)
            fw_copy(sign, t, part_of(sign, first), m, core).start()

    for m, (t, first) in enumerate(trips):
        for sign in (1, -1):
            fw_copy(sign, t, part_of(sign, first), m, core).wait_send()
            fw_copy(sign, t, part_of(sign, first), m, 1 - core).wait_recv()
    own_forward(core).wait_send()
    own_forward(1 - core).wait_recv()
    own.wait()
    for copy in sent:
        copy.wait_send()
    for r in order:
        raw[r].wait_send()
    for sign in (1, -1):
        for m in range(count):
            for copy in q_copies(sign, m):
                copy.wait_send()
    for copy in idx_copies + pick_copies:
        copy.wait_send()


def local(n_group, n_shard, gradients, momentum, master, indices):
    rows, width = master.shape
    whole = gradients.shape[3]
    n = n_shard // 2
    steps = n // 2
    count = 2 * steps - 1
    height = rows // BLOCK
    slots = indices.shape[2] * indices.shape[3]
    pad = -(-height // 8) * 8
    idx = jnp.pad(indices[0].reshape(height, slots), ((0, pad - height), (0, 0)))
    span = 256 if width % 256 == 0 else 128
    table = cosine_table(BLOCK)
    rt = np.kron(np.eye(height), table).astype(np.float32)
    ct = np.kron(np.eye(span // BLOCK), table).astype(np.float32)
    others = max(n_group - 1, 1)
    dma = pltpu.SemaphoreType.DMA
    vmem = pl.BlockSpec(memory_space=pltpu.VMEM)
    hbm = pl.BlockSpec(memory_space=pl.ANY)
    body = functools.partial(kernel, n_group, n, width, 0)
    return pl.pallas_call(
        body,
        out_shape=(
            jax.ShapeDtypeStruct((1, rows, width), F32),
            jax.ShapeDtypeStruct((rows, width), F32),
            jax.ShapeDtypeStruct((rows, whole), BF16),
        ),
        in_specs=[hbm] + [vmem] * 6,
        out_specs=(vmem, vmem, hbm),
        scratch_shapes=[
            pltpu.VMEM((n, rows, width), BF16),
            pltpu.VMEM((n, rows, width), BF16),
            pltpu.VMEM((2, count, rows // 2, width), jnp.int16),
            pltpu.VMEM((2, count, rows // 2, width), jnp.int16),
            pltpu.VMEM((2, count, 8, LANES), F32),
            pltpu.VMEM((2, count, 8, LANES), F32),
            pltpu.VMEM((rows, width), F32),
            pltpu.VMEM((width, rows), F32),
            pltpu.VMEM((rows, width), F32),
            pltpu.VMEM((rows, width), F32),
            pltpu.VMEM((rows, width), BF16),
            pltpu.VMEM((others, pad, slots), jnp.int32),
            pltpu.VMEM((n_group, pad, slots), F32),
            dma((n,)), dma((n,)), dma((n,)),
            dma((2, count)), dma((2, count)), dma((2, count)), dma((2, count)),
            dma((others,)), dma((others,)), dma((others,)), dma((others,)),
            dma, dma((2, count)), dma((2, count)), dma((2, count + 1)), dma((2, count + 1)),
        ],
        compiler_params=pltpu.CompilerParams(
            collective_id=0, has_side_effects=True, vmem_limit_bytes=44 * 1024 * 1024),
        cost_estimate=pl.CostEstimate(
            flops=30 * rows * rows * width, bytes_accessed=4 * rows * whole, transcendentals=rows * width),
    )(gradients, momentum, master, idx, jnp.asarray(rt), jnp.asarray(rt.T.copy()), jnp.asarray(ct))


def solution(mesh):
    placed = (
        P("group", "shard", None, None),
        P("group", None, "shard"),
        P(None, "shard"),
        P("group", None, "shard", None),
    )
    return jax.shard_map(
        functools.partial(local, mesh.shape["group"], mesh.shape["shard"]),
        mesh=mesh,
        in_specs=placed,
        out_specs=(P("group", None, "shard"), P(None, "shard"), P()),
        check_vma=False,
    )
```

```python
import functools

import jax
import jax.numpy as jnp
import numpy as np
from jax import lax
from jax.experimental import pallas as pl
from jax.experimental.pallas import tpu as pltpu
from jax.sharding import PartitionSpec as P

BLOCK = 64
LANES = 128
TOP = 32767.0

momentum_decay = 0.9
step_rate = 0.5

HI = lax.Precision.HIGHEST
MESH = pl.DeviceIdType.MESH
F32 = jnp.float32
BF16 = jnp.bfloat16


def cosine_table(side):
    freqs = np.arange(side, dtype=np.float64)[:, None]
    places = np.arange(side, dtype=np.float64)[None, :]
    table = np.cos(np.pi * (2.0 * places + 1.0) * freqs / (2.0 * side))
    weights = np.where(freqs == 0.0, np.sqrt(1.0 / side), np.sqrt(2.0 / side))
    return table * weights


def split3(x):
    high = x.astype(BF16)
    rest = x - high.astype(F32)
    mid = rest.astype(BF16)
    low = (rest - mid.astype(F32)).astype(BF16)
    return high, mid, low


def dot(a, b):
    return jnp.dot(a, b, precision=HI, preferred_element_type=F32)


def dot_nt(a, b, precision=None):
    return lax.dot_general(a, b, (((1,), (1,)), ((), ())), precision=precision, preferred_element_type=F32)


def kernel(n_group, n, width,
           grad, mom_hbm, master_hbm, idx_hbm, rt_hbm, rtt_hbm, ct_hbm,
           mom_out, master_out, params_out,
           mine, sib, sendq, recvq, sends, recvs, acc, dense, param, idx_raw, idx, pick_all,
           mom, master, rt, rtt, ct,
           mine_sem, raw_send, raw_recv, q_send, q_recv, s_send, s_recv,
           idx_send, idx_recv, pick_send, pick_recv, load_sem,
           own_sem, ag_send, ag_recv, fw_send, fw_recv, y_send, y_recv, fy_send, fy_recv):
    rows = master.shape[0]
    half = rows // 2
    quarter = half // 2
    lines = half // BLOCK
    steps = n // 2
    count = 2 * steps - 1
    across = width // BLOCK
    slots = idx.shape[2]
    per_block = slots // across
    paired = n_group % 2 == 0
    shared = half // 4 if paired else 0
    sub = (half - shared) // 2

    g = lax.axis_index("group")
    s = lax.axis_index("shard")
    core = lax.rem(s, 2)
    chip = s // 2
    odd = lax.rem(chip, 2)
    pos = (1 - odd) * (chip // 2) + odd * (n - 1 - chip // 2)
    parity = lax.rem(g, 2)
    partner = g + 1 - 2 * parity

    def chip_at(offset):
        place = lax.rem(pos + (offset % n), n)
        back = place // (n // 2)
        return (1 - back) * (2 * place) + back * (2 * (n - 1 - place) + 1)

    sibling = 2 * chip + (1 - core)
    beside = {1: 2 * chip_at(1) + core, -1: 2 * chip_at(-1) + core}

    def columns(shard):
        return pl.ds(pl.multiple_of(shard * width, LANES), width)

    def other_group(k):
        return lax.rem(g + k, n_group)

    def side(sign):
        return 0 if sign == 1 else 1

    barrier = pltpu.get_barrier_semaphore()
    for sign in (1, -1):
        pl.semaphore_signal(barrier, inc=1, device_id={"shard": beside[sign]}, device_id_type=MESH)
    pl.semaphore_signal(barrier, inc=1, device_id={"shard": sibling}, device_id_type=MESH)
    for k in range(1, n_group):
        pl.semaphore_signal(barrier, inc=1, device_id={"group": other_group(k)}, device_id_type=MESH)

    order = [steps]
    for t in range(1, steps):
        order += [steps - t, n - (steps - t)]
    order += [0]

    own_loads = {}
    for r in order:
        own_loads[r] = pltpu.make_async_copy(
            grad.at[0, 0, :, columns(2 * chip_at(r) + core)], mine.at[r], mine_sem.at[r])
        own_loads[r].start()
    operands = []
    for i, (there, here) in enumerate((
            (idx_hbm, idx_raw.at[0]), (mom_hbm.at[0], mom), (rt_hbm, rt), (ct_hbm, ct),
            (rtt_hbm, rtt), (master_hbm, master))):
        copy = pltpu.make_async_copy(there, here, load_sem.at[i])
        copy.start()
        operands.append(copy)

    pl.semaphore_wait(barrier, 3 + n_group - 1)

    raw = {}
    for r in order:
        raw[r] = pltpu.make_async_remote_copy(
            src_ref=grad.at[0, 0, :, columns(2 * chip_at(r) + 1 - core)], dst_ref=sib.at[r],
            send_sem=raw_send.at[r], recv_sem=raw_recv.at[r],
            device_id={"shard": sibling}, device_id_type=MESH)
        raw[r].start()

    idx_copies = []
    for k in range(1, n_group):
        copy = pltpu.make_async_remote_copy(
            src_ref=idx_hbm, dst_ref=idx_raw.at[k],
            send_sem=idx_send.at[k - 1], recv_sem=idx_recv.at[k - 1],
            device_id={"group": other_group(k)}, device_id_type=MESH)
        copy.start()
        idx_copies.append(copy)

    def lay_indices(k):
        for a in range(rows // BLOCK):
            idx[k, a:a + 1, :] = jnp.concatenate(
                [idx_raw[k, a * across + b:a * across + b + 1, :] for b in range(across)], axis=1)

    def part_of(sign, first):
        return side(sign) if first else 1 - side(sign)

    ready = set()

    def arrived(r):
        if r not in ready:
            ready.add(r)
            own_loads[r].wait()
            raw[r].wait_recv()

    def q_copies(p, sign, m):
        d = 2 * p + side(sign)
        there = {"shard": beside[sign]}
        return (
            pltpu.make_async_remote_copy(
                src_ref=sendq.at[d, m], dst_ref=recvq.at[d, m],
                send_sem=q_send.at[d, m], recv_sem=q_recv.at[d, m],
                device_id=there, device_id_type=MESH),
            pltpu.make_async_remote_copy(
                src_ref=sends.at[d, m], dst_ref=recvs.at[d, m],
                send_sem=s_send.at[d, m], recv_sem=s_recv.at[d, m],
                device_id=there, device_id_type=MESH))

    def message(t, first):
        return 0 if t == 0 else 2 * t - 1 + (1 if first else 0)

    def received(d, m, lane):
        scale = recvs[d, m, 0:1, :]
        return recvq[d, m, :, pl.ds(lane * LANES, LANES)].astype(jnp.int32).astype(F32) * scale

    tiles = width // LANES

    def sum_step(p, t, first):
        for sign in (1, -1):
            d = 2 * p + side(sign)
            r = (sign * (steps - t)) % n
            m = message(t, first)
            arrived(r)
            has = t >= 2 or (t == 1 and first)
            if has:
                before = message(t - 1, first)
                for copy in q_copies(p, sign, before):
                    copy.wait_recv()
            band = pl.ds(p * half + part_of(sign, first) * quarter, quarter)
            values = []
            top = None
            for lane in range(tiles):
                cols = pl.ds(lane * LANES, LANES)
                x = mine[r, band, cols].astype(F32) + sib[r, band, cols].astype(F32)
                if has:
                    x = x + received(d, before, lane)
                values.append(x)
                peak = jnp.max(jnp.abs(x), axis=0, keepdims=True)
                top = peak if top is None else jnp.maximum(top, peak)
            top = jnp.maximum(top, 1e-30)
            inverse = TOP / top
            for lane in range(tiles):
                q = jnp.round(values[lane] * inverse).astype(jnp.int32).astype(jnp.int16)
                sendq[d, m, :, pl.ds(lane * LANES, LANES)] = q
            sends[d, m] = jnp.broadcast_to(top * (1.0 / TOP), (8, LANES))
            for copy in q_copies(p, sign, m):
                copy.start()

    def sum_end(p):
        arrived(0)
        for first in (False, True):
            for sign in (1, -1):
                for copy in q_copies(p, sign, message(steps - 1, first)):
                    copy.wait_recv()
        for part in range(2):
            band = pl.ds(p * half + part * quarter, quarter)
            for lane in range(tiles):
                cols = pl.ds(lane * LANES, LANES)
                x = mine[0, band, cols].astype(F32) + sib[0, band, cols].astype(F32)
                for sign in (1, -1):
                    x = x + received(2 * p + side(sign), message(steps - 1, part == side(sign)), lane)
                acc[band, cols] = momentum_decay * mom[band, cols] + x

    span = ct.shape[0]
    lane_block = lax.broadcasted_iota(jnp.int32, (1, slots), 1) // per_block

    def row_hot(ids):
        return lax.broadcasted_iota(jnp.int32, (BLOCK, slots), 0) == (ids >> 6)

    def col_hot(ids):
        places = lane_block * BLOCK + (ids & (BLOCK - 1))
        return lax.broadcasted_iota(jnp.int32, (width, slots), 0) == places

    def spread(ids, picked):
        hot = jnp.where(row_hot(ids), picked, 0.0)
        cols = jnp.where(col_hot(ids), 1.0, 0.0).astype(BF16)
        high, mid, low = split3(hot)
        return dot_nt(high, cols) + (dot_nt(mid, cols) + dot_nt(low, cols))

    def pick_copy(p, k):
        return pltpu.make_async_remote_copy(
            src_ref=pick_all.at[0, p], dst_ref=pick_all.at[k, p],
            send_sem=pick_send.at[p, k - 1], recv_sem=pick_recv.at[p, k - 1],
            device_id={"group": other_group(k)}, device_id_type=MESH)

    def forward(p):
        stage = dot(rt[...], acc[pl.ds(p * half, half), :])
        pieces = []
        for tile in range(width // span):
            pieces.append(dot_nt(ct[...], stage[:, tile * span:(tile + 1) * span], HI))
        high, mid, low = split3(jnp.concatenate(pieces, axis=0))
        pick_all[0, p] = jnp.zeros(pick_all.shape[2:], F32)
        for a in range(lines):
            line = p * lines + a
            ids = idx[0, line:line + 1, :]
            hot = lax.broadcasted_iota(jnp.int32, (half, slots), 0) == (ids >> 6) + a * BLOCK
            hot = jnp.where(hot, 1.0, 0.0).astype(BF16)
            at_row = (jnp.dot(high, hot, preferred_element_type=F32)
                      + (jnp.dot(mid, hot, preferred_element_type=F32)
                         + jnp.dot(low, hot, preferred_element_type=F32)))
            pick_all[0, p, a:a + 1, :] = jnp.sum(jnp.where(col_hot(ids), at_row, 0.0), axis=0, keepdims=True)
        for k in range(1, n_group):
            pick_copy(p, k).start()
        for a in range(lines):
            line = p * lines + a
            dense[pl.ds(line * BLOCK, BLOCK), :] = spread(idx[0, line:line + 1, :], pick_all[0, p, a:a + 1, :])

    def back(field, tile):
        return dot(field[:, tile * span:(tile + 1) * span], ct[...])

    def update(p):
        for k in range(1, n_group):
            pick_copy(p, k).wait_recv()
        bands = []
        for a in range(lines):
            line = p * lines + a
            band = dense[pl.ds(line * BLOCK, BLOCK), :]
            for k in range(1, n_group):
                band = band + spread(idx[k, line:line + 1, :], pick_all[k, p, a:a + 1, :])
            bands.append(band)
        stage = dot(rtt[...], jnp.concatenate(bands, axis=0))
        here = pl.ds(p * half, half)
        for tile in range(width // span):
            cols = pl.ds(tile * span, span)
            new = master[here, cols] - step_rate * jnp.tanh(back(stage, tile))
            master_out[here, cols] = new
            param[here, cols] = new.astype(BF16)

    def momentum_half(p):
        here = pl.ds(p * half, half)
        stage = dot(rtt[...], dense[here, :])
        for tile in range(width // span):
            cols = pl.ds(tile * span, span)
            mom_out[0, here, cols] = acc[here, cols] - back(stage, tile)

    def place(offset):
        return columns(2 * chip_at(offset) + core)

    def ring_rows(p, part):
        return pl.ds(pl.multiple_of(p * half + parity * shared + part * sub, 16), sub)

    def ag_copy(p, sign, t, first):
        d = 2 * p + side(sign)
        m = number[(t, first)]
        band = ring_rows(p, part_of(sign, first))
        where = params_out.at[band, place(-sign * t)]
        return pltpu.make_async_remote_copy(
            src_ref=param.at[band, :] if t == 0 else where, dst_ref=where,
            send_sem=ag_send.at[d, m], recv_sem=ag_recv.at[d, m],
            device_id={"shard": beside[sign]}, device_id_type=MESH)

    def ag_arrival(p, sign, t, first):
        d = 2 * p + side(sign)
        m = number[(t, first)]
        where = params_out.at[ring_rows(p, part_of(sign, first)), place(-sign * (t + 1))]
        return pltpu.make_async_remote_copy(
            src_ref=where, dst_ref=where,
            send_sem=ag_send.at[d, m], recv_sem=ag_recv.at[d, m],
            device_id={"shard": beside[sign]}, device_id_type=MESH)

    def fw_copy(p, sign, t, first, c):
        d = 2 * p + side(sign)
        m = number[(t, first)]
        where = params_out.at[ring_rows(p, part_of(sign, first)), columns(2 * chip_at(-sign * (t + 1)) + c)]
        return pltpu.make_async_remote_copy(
            src_ref=where, dst_ref=where,
            send_sem=fw_send.at[d, m], recv_sem=fw_recv.at[d, m],
            device_id={"shard": sibling}, device_id_type=MESH)

    def y_number(sign, t):
        return 2 * (steps - 1) if t == steps - 1 else t + side(sign) * (steps - 1)

    def y_rows(p, which):
        return pl.ds(pl.multiple_of(p * half + which * (half - shared), 16), shared)

    def y_copy(p, sign, t, which):
        where = params_out.at[y_rows(p, which), place(-sign * (t + 1))]
        i = y_number(sign, t)
        return pltpu.make_async_remote_copy(
            src_ref=where, dst_ref=where,
            send_sem=y_send.at[p, i], recv_sem=y_recv.at[p, i],
            device_id={"group": partner}, device_id_type=MESH)

    def fy_copy(p, sign, t, c):
        where = params_out.at[y_rows(p, 1 - parity), columns(2 * chip_at(-sign * (t + 1)) + c)]
        i = y_number(sign, t)
        return pltpu.make_async_remote_copy(
            src_ref=where, dst_ref=where,
            send_sem=fy_send.at[p, i], recv_sem=fy_recv.at[p, i],
            device_id={"shard": sibling}, device_id_type=MESH)

    trips = [(t, first) for t in range(steps) for first in ((True, False) if t < steps - 1 else (True,))]
    number = {trip: m for m, trip in enumerate(trips)}

    def own_copy(p):
        here = pl.ds(p * half, half)
        return pltpu.make_async_copy(param.at[here, :], params_out.at[here, place(0)], own_sem.at[p])

    def own_forward(p, c):
        here = pl.ds(p * half, half)
        return pltpu.make_async_remote_copy(
            src_ref=param.at[here, :], dst_ref=params_out.at[here, columns(2 * chip + c)],
            send_sem=fw_send.at[2 * p, count], recv_sem=fw_recv.at[2 * p, count],
            device_id={"shard": sibling}, device_id_type=MESH)

    sent = []
    pending = []
    y_done = []

    def go(p, sign, t, first):
        if (t, first) in number:
            copy = ag_copy(p, sign, t, first)
            copy.start()
            sent.append(copy)

    def gather_start(p):
        for first in (True, False):
            for sign in (1, -1):
                go(p, sign, 0, first)
        own_copy(p).start()
        own_forward(p, core).start()

    def y_take():
        p, sign, t = pending.pop(0)
        y_copy(p, sign, t, 1 - parity).wait_recv()
        fy_copy(p, sign, t, core).start()
        y_done.append((p, sign, t))

    def y_give(p, sign, t):
        if paired:
            y_copy(p, sign, t, parity).start()
            pending.append((p, sign, t))

    def gather_event(p, t, first):
        for sign in (1, -1):
            ag_arrival(p, sign, t, first).wait_recv()
            go(p, sign, t + 1, first)
            fw_copy(p, sign, t, first, core).start()
            if not first:
                y_give(p, sign, t)
        if t == steps - 1:
            y_give(p, 1, t)
        while len(pending) > 3:
            y_take()

    waves = [(0, True)]
    for t in range(1, steps):
        waves += [(t, False), (t, True)]
    sum_step(0, *waves[0])
    sum_step(0, *waves[1])
    for copy in operands:
        copy.wait()
    lay_indices(0)
    for wave in waves[2:]:
        sum_step(0, *wave)
    for wave in waves[:2]:
        sum_step(1, *wave)
    sum_end(0)
    forward(0)
    for wave in waves[2:-2]:
        sum_step(1, *wave)
    for k in range(1, n_group):
        idx_copies[k - 1].wait_recv()
        lay_indices(k)
    update(0)
    for wave in waves[-2:]:
        sum_step(1, *wave)
    gather_start(0)
    sum_end(1)
    forward(1)
    for trip in trips[:2]:
        gather_event(0, *trip)
    update(1)
    gather_start(1)
    momentum_half(0)
    left = trips[2:]
    others = list(trips)
    turn = 0
    while left or others:
        for trip in left[:2]:
            gather_event(0, *trip)
        left = left[2:]
        for trip in others[:2]:
            gather_event(1, *trip)
        others = others[2:]
        if turn == 0:
            momentum_half(1)
        turn += 1
    while pending:
        y_take()

    for p in range(2):
        for t, first in trips:
            for sign in (1, -1):
                fw_copy(p, sign, t, first, core).wait_send()
                fw_copy(p, sign, t, first, 1 - core).wait_recv()
        own_forward(p, core).wait_send()
        own_forward(p, 1 - core).wait_recv()
        own_copy(p).wait()
    for p, sign, t in y_done:
        y_copy(p, sign, t, parity).wait_send()
        fy_copy(p, sign, t, core).wait_send()
        fy_copy(p, sign, t, 1 - core).wait_recv()
    for copy in sent:
        copy.wait_send()
    for r in order:
        raw[r].wait_send()
    for p in range(2):
        for sign in (1, -1):
            for m in range(count):
                for copy in q_copies(p, sign, m):
                    copy.wait_send()
        for k in range(1, n_group):
            pick_copy(p, k).wait_send()
    for copy in idx_copies:
        copy.wait_send()


def local(n_group, n_shard, gradients, momentum, master, indices):
    rows, width = master.shape
    whole = gradients.shape[3]
    n = n_shard // 2
    steps = n // 2
    count = 2 * steps - 1
    height = rows // BLOCK
    slots = indices.shape[2] * indices.shape[3]
    idx = indices.reshape(-1, indices.shape[3])
    span = 256 if width % 256 == 0 else 128
    table = cosine_table(BLOCK)
    rt = np.kron(np.eye(height // 2), table).astype(np.float32)
    ct = np.kron(np.eye(span // BLOCK), table).astype(np.float32)
    others = max(n_group - 1, 1)
    dma = pltpu.SemaphoreType.DMA
    vmem = pl.BlockSpec(memory_space=pltpu.VMEM)
    hbm = pl.BlockSpec(memory_space=pltpu.HBM)
    free = pl.BlockSpec(memory_space=pl.ANY)
    body = functools.partial(kernel, n_group, n, width)
    return pl.pallas_call(
        body,
        out_shape=(
            jax.ShapeDtypeStruct((1, rows, width), F32),
            jax.ShapeDtypeStruct((rows, width), F32),
            jax.ShapeDtypeStruct((rows, whole), BF16),
        ),
        in_specs=[hbm] * 7,
        out_specs=(vmem, vmem, free),
        scratch_shapes=[
            pltpu.VMEM((n, rows, width), BF16),
            pltpu.VMEM((n, rows, width), BF16),
            pltpu.VMEM((4, count, rows // 4, width), jnp.int16),
            pltpu.VMEM((4, count, rows // 4, width), jnp.int16),
            pltpu.VMEM((4, count, 8, LANES), F32),
            pltpu.VMEM((4, count, 8, LANES), F32),
            pltpu.VMEM((rows, width), F32),
            pltpu.VMEM((rows, width), F32),
            pltpu.VMEM((rows, width), BF16),
            pltpu.VMEM((n_group,) + idx.shape, jnp.int32),
            pltpu.VMEM((n_group, -(-height // 8) * 8, slots), jnp.int32),
            pltpu.VMEM((n_group, 2, 8, slots), F32),
            pltpu.VMEM((rows, width), F32),
            pltpu.VMEM((rows, width), F32),
            pltpu.VMEM(rt.shape, F32),
            pltpu.VMEM(rt.shape, F32),
            pltpu.VMEM(ct.shape, F32),
            dma((n,)), dma((n,)), dma((n,)),
            dma((4, count)), dma((4, count)), dma((4, count)), dma((4, count)),
            dma((others,)), dma((others,)), dma((2, others)), dma((2, others)), dma((6,)),
            dma((2,)), dma((4, count)), dma((4, count)), dma((4, count + 1)), dma((4, count + 1)),
            dma((2, count)), dma((2, count)), dma((2, count)), dma((2, count)),
        ],
        compiler_params=pltpu.CompilerParams(
            collective_id=0, has_side_effects=True, vmem_limit_bytes=44 * 1024 * 1024),
        cost_estimate=pl.CostEstimate(
            flops=30 * rows * rows * width, bytes_accessed=4 * rows * whole, transcendentals=rows * width),
    )(gradients, momentum, master, idx, jnp.asarray(rt), jnp.asarray(rt.T.copy()), jnp.asarray(ct))


def solution(mesh):
    placed = (
        P("group", "shard", None, None),
        P("group", None, "shard"),
        P(None, "shard"),
        P("group", None, "shard", None),
    )
    return jax.shard_map(
        functools.partial(local, mesh.shape["group"], mesh.shape["shard"]),
        mesh=mesh,
        in_specs=placed,
        out_specs=(P("group", None, "shard"), P(None, "shard"), P()),
        check_vma=False,
    )
```

```python
import functools

import jax
import jax.numpy as jnp
import numpy as np
from jax import lax
from jax.experimental import pallas as pl
from jax.experimental.pallas import tpu as pltpu
from jax.sharding import PartitionSpec as P

BLOCK = 64
LANES = 128
TOP = 32767.0

momentum_decay = 0.9
step_rate = 0.5

HI = lax.Precision.HIGHEST
MESH = pl.DeviceIdType.MESH
F32 = jnp.float32
BF16 = jnp.bfloat16


def cosine_table(side):
    freqs = np.arange(side, dtype=np.float64)[:, None]
    places = np.arange(side, dtype=np.float64)[None, :]
    table = np.cos(np.pi * (2.0 * places + 1.0) * freqs / (2.0 * side))
    weights = np.where(freqs == 0.0, np.sqrt(1.0 / side), np.sqrt(2.0 / side))
    return table * weights


def split3(x):
    high = x.astype(BF16)
    rest = x - high.astype(F32)
    mid = rest.astype(BF16)
    low = (rest - mid.astype(F32)).astype(BF16)
    return high, mid, low


def dot(a, b):
    return jnp.dot(a, b, precision=HI, preferred_element_type=F32)


def dot_nt(a, b, precision=None):
    return lax.dot_general(a, b, (((1,), (1,)), ((), ())), precision=precision, preferred_element_type=F32)


def kernel(n_group, n, width,
           grad, mom_hbm, master_hbm, idx_hbm, rt_hbm, rtt_hbm, ct_hbm,
           mom_out, master_out, params_out,
           mine, sib, sendq, recvq, sends, recvs, acc, dense, param, idx_raw, idx, pick_all,
           mom, master, rt, rtt, ct,
           mine_sem, raw_send, raw_recv, q_send, q_recv, s_send, s_recv,
           idx_send, idx_recv, pick_send, pick_recv, load_sem,
           own_sem, ag_send, ag_recv, fw_send, fw_recv, y_send, y_recv, fy_send, fy_recv):
    rows = master.shape[0]
    half = rows // 2
    quarter = half // 2
    lines = half // BLOCK
    steps = n // 2
    count = 2 * steps - 1
    across = width // BLOCK
    slots = idx.shape[2]
    per_block = slots // across
    paired = False
    shared = half // 4 if paired else 0
    sub = (half - shared) // 2

    g = lax.axis_index("group")
    s = lax.axis_index("shard")
    core = lax.rem(s, 2)
    chip = s // 2
    odd = lax.rem(chip, 2)
    pos = (1 - odd) * (chip // 2) + odd * (n - 1 - chip // 2)
    parity = lax.rem(g, 2)
    partner = g + 1 - 2 * parity

    def chip_at(offset):
        place = lax.rem(pos + (offset % n), n)
        back = place // (n // 2)
        return (1 - back) * (2 * place) + back * (2 * (n - 1 - place) + 1)

    sibling = 2 * chip + (1 - core)
    beside = {1: 2 * chip_at(1) + core, -1: 2 * chip_at(-1) + core}

    def columns(shard):
        return pl.ds(pl.multiple_of(shard * width, LANES), width)

    def other_group(k):
        return lax.rem(g + k, n_group)

    def side(sign):
        return 0 if sign == 1 else 1

    barrier = pltpu.get_barrier_semaphore()
    for sign in (1, -1):
        pl.semaphore_signal(barrier, inc=1, device_id={"shard": beside[sign]}, device_id_type=MESH)
    pl.semaphore_signal(barrier, inc=1, device_id={"shard": sibling}, device_id_type=MESH)
    for k in range(1, n_group):
        pl.semaphore_signal(barrier, inc=1, device_id={"group": other_group(k)}, device_id_type=MESH)

    order = [steps]
    for t in range(1, steps):
        order += [steps - t, n - (steps - t)]
    order += [0]

    own_loads = {}
    for r in order:
        own_loads[r] = pltpu.make_async_copy(
            grad.at[0, 0, :, columns(2 * chip_at(r) + core)], mine.at[r], mine_sem.at[r])
        own_loads[r].start()
    operands = []
    for i, (there, here) in enumerate((
            (idx_hbm, idx_raw.at[0]), (mom_hbm.at[0], mom), (rt_hbm, rt), (ct_hbm, ct),
            (rtt_hbm, rtt), (master_hbm, master))):
        copy = pltpu.make_async_copy(there, here, load_sem.at[i])
        copy.start()
        operands.append(copy)

    pl.semaphore_wait(barrier, 3 + n_group - 1)

    raw = {}
    for r in order:
        raw[r] = pltpu.make_async_remote_copy(
            src_ref=grad.at[0, 0, :, columns(2 * chip_at(r) + 1 - core)], dst_ref=sib.at[r],
            send_sem=raw_send.at[r], recv_sem=raw_recv.at[r],
            device_id={"shard": sibling}, device_id_type=MESH)
        raw[r].start()

    idx_copies = []
    for k in range(1, n_group):
        copy = pltpu.make_async_remote_copy(
            src_ref=idx_hbm, dst_ref=idx_raw.at[k],
            send_sem=idx_send.at[k - 1], recv_sem=idx_recv.at[k - 1],
            device_id={"group": other_group(k)}, device_id_type=MESH)
        copy.start()
        idx_copies.append(copy)

    def lay_indices(k):
        for a in range(rows // BLOCK):
            idx[k, a:a + 1, :] = jnp.concatenate(
                [idx_raw[k, a * across + b:a * across + b + 1, :] for b in range(across)], axis=1)

    def part_of(sign, first):
        return side(sign) if first else 1 - side(sign)

    ready = set()

    def arrived(r):
        if r not in ready:
            ready.add(r)
            own_loads[r].wait()
            raw[r].wait_recv()

    def q_copies(p, sign, m):
        d = 2 * p + side(sign)
        there = {"shard": beside[sign]}
        return (
            pltpu.make_async_remote_copy(
                src_ref=sendq.at[d, m], dst_ref=recvq.at[d, m],
                send_sem=q_send.at[d, m], recv_sem=q_recv.at[d, m],
                device_id=there, device_id_type=MESH),
            pltpu.make_async_remote_copy(
                src_ref=sends.at[d, m], dst_ref=recvs.at[d, m],
                send_sem=s_send.at[d, m], recv_sem=s_recv.at[d, m],
                device_id=there, device_id_type=MESH))

    def message(t, first):
        return 0 if t == 0 else 2 * t - 1 + (1 if first else 0)

    def received(d, m, lane):
        scale = recvs[d, m, 0:1, :]
        return recvq[d, m, :, pl.ds(lane * LANES, LANES)].astype(jnp.int32).astype(F32) * scale

    tiles = width // LANES

    def sum_step(p, t, first):
        for sign in (1, -1):
            d = 2 * p + side(sign)
            r = (sign * (steps - t)) % n
            m = message(t, first)
            arrived(r)
            has = t >= 2 or (t == 1 and first)
            if has:
                before = message(t - 1, first)
                for copy in q_copies(p, sign, before):
                    copy.wait_recv()
            band = pl.ds(p * half + part_of(sign, first) * quarter, quarter)
            values = []
            top = None
            for lane in range(tiles):
                cols = pl.ds(lane * LANES, LANES)
                x = mine[r, band, cols].astype(F32) + sib[r, band, cols].astype(F32)
                if has:
                    x = x + received(d, before, lane)
                values.append(x)
                peak = jnp.max(jnp.abs(x), axis=0, keepdims=True)
                top = peak if top is None else jnp.maximum(top, peak)
            top = jnp.maximum(top, 1e-30)
            inverse = TOP / top
            for lane in range(tiles):
                q = jnp.round(values[lane] * inverse).astype(jnp.int32).astype(jnp.int16)
                sendq[d, m, :, pl.ds(lane * LANES, LANES)] = q
            sends[d, m] = jnp.broadcast_to(top * (1.0 / TOP), (8, LANES))
            for copy in q_copies(p, sign, m):
                copy.start()

    def sum_end(p):
        arrived(0)
        for first in (False, True):
            for sign in (1, -1):
                for copy in q_copies(p, sign, message(steps - 1, first)):
                    copy.wait_recv()
        for part in range(2):
            band = pl.ds(p * half + part * quarter, quarter)
            for lane in range(tiles):
                cols = pl.ds(lane * LANES, LANES)
                x = mine[0, band, cols].astype(F32) + sib[0, band, cols].astype(F32)
                for sign in (1, -1):
                    x = x + received(2 * p + side(sign), message(steps - 1, part == side(sign)), lane)
                acc[band, cols] = momentum_decay * mom[band, cols] + x

    span = ct.shape[0]
    lane_block = lax.broadcasted_iota(jnp.int32, (1, slots), 1) // per_block

    def row_hot(ids):
        return lax.broadcasted_iota(jnp.int32, (BLOCK, slots), 0) == (ids >> 6)

    def col_hot(ids):
        places = lane_block * BLOCK + (ids & (BLOCK - 1))
        return lax.broadcasted_iota(jnp.int32, (width, slots), 0) == places

    def spread(ids, picked):
        hot = jnp.where(row_hot(ids), picked, 0.0)
        cols = jnp.where(col_hot(ids), 1.0, 0.0).astype(BF16)
        high, mid, low = split3(hot)
        return dot_nt(high, cols) + (dot_nt(mid, cols) + dot_nt(low, cols))

    def pick_copy(p, k):
        return pltpu.make_async_remote_copy(
            src_ref=pick_all.at[0, p], dst_ref=pick_all.at[k, p],
            send_sem=pick_send.at[p, k - 1], recv_sem=pick_recv.at[p, k - 1],
            device_id={"group": other_group(k)}, device_id_type=MESH)

    def forward(p):
        stage = dot(rt[...], acc[pl.ds(p * half, half), :])
        pieces = []
        for tile in range(width // span):
            pieces.append(dot_nt(ct[...], stage[:, tile * span:(tile + 1) * span], HI))
        high, mid, low = split3(jnp.concatenate(pieces, axis=0))
        pick_all[0, p] = jnp.zeros(pick_all.shape[2:], F32)
        for a in range(lines):
            line = p * lines + a
            ids = idx[0, line:line + 1, :]
            hot = lax.broadcasted_iota(jnp.int32, (half, slots), 0) == (ids >> 6) + a * BLOCK
            hot = jnp.where(hot, 1.0, 0.0).astype(BF16)
            at_row = (jnp.dot(high, hot, preferred_element_type=F32)
                      + (jnp.dot(mid, hot, preferred_element_type=F32)
                         + jnp.dot(low, hot, preferred_element_type=F32)))
            pick_all[0, p, a:a + 1, :] = jnp.sum(jnp.where(col_hot(ids), at_row, 0.0), axis=0, keepdims=True)
        for k in range(1, n_group):
            pick_copy(p, k).start()
        for a in range(lines):
            line = p * lines + a
            dense[pl.ds(line * BLOCK, BLOCK), :] = spread(idx[0, line:line + 1, :], pick_all[0, p, a:a + 1, :])

    def back(field, tile):
        return dot(field[:, tile * span:(tile + 1) * span], ct[...])

    def update(p):
        for k in range(1, n_group):
            pick_copy(p, k).wait_recv()
        bands = []
        for a in range(lines):
            line = p * lines + a
            band = dense[pl.ds(line * BLOCK, BLOCK), :]
            for k in range(1, n_group):
                band = band + spread(idx[k, line:line + 1, :], pick_all[k, p, a:a + 1, :])
            bands.append(band)
        stage = dot(rtt[...], jnp.concatenate(bands, axis=0))
        here = pl.ds(p * half, half)
        for tile in range(width // span):
            cols = pl.ds(tile * span, span)
            new = master[here, cols] - step_rate * jnp.tanh(back(stage, tile))
            master_out[here, cols] = new
            param[here, cols] = new.astype(BF16)

    def momentum_half(p):
        here = pl.ds(p * half, half)
        stage = dot(rtt[...], dense[here, :])
        for tile in range(width // span):
            cols = pl.ds(tile * span, span)
            mom_out[0, here, cols] = acc[here, cols] - back(stage, tile)

    def place(offset):
        return columns(2 * chip_at(offset) + core)

    def ring_rows(p, part):
        return pl.ds(pl.multiple_of(p * half + parity * shared + part * sub, 16), sub)

    def ag_copy(p, sign, t, first):
        d = 2 * p + side(sign)
        m = number[(t, first)]
        band = ring_rows(p, part_of(sign, first))
        where = params_out.at[band, place(-sign * t)]
        return pltpu.make_async_remote_copy(
            src_ref=param.at[band, :] if t == 0 else where, dst_ref=where,
            send_sem=ag_send.at[d, m], recv_sem=ag_recv.at[d, m],
            device_id={"shard": beside[sign]}, device_id_type=MESH)

    def ag_arrival(p, sign, t, first):
        d = 2 * p + side(sign)
        m = number[(t, first)]
        where = params_out.at[ring_rows(p, part_of(sign, first)), place(-sign * (t + 1))]
        return pltpu.make_async_remote_copy(
            src_ref=where, dst_ref=where,
            send_sem=ag_send.at[d, m], recv_sem=ag_recv.at[d, m],
            device_id={"shard": beside[sign]}, device_id_type=MESH)

    def fw_copy(p, sign, t, first, c):
        d = 2 * p + side(sign)
        m = number[(t, first)]
        where = params_out.at[ring_rows(p, part_of(sign, first)), columns(2 * chip_at(-sign * (t + 1)) + c)]
        return pltpu.make_async_remote_copy(
            src_ref=where, dst_ref=where,
            send_sem=fw_send.at[d, m], recv_sem=fw_recv.at[d, m],
            device_id={"shard": sibling}, device_id_type=MESH)

    def y_number(sign, t):
        return 2 * (steps - 1) if t == steps - 1 else t + side(sign) * (steps - 1)

    def y_rows(p, which):
        return pl.ds(pl.multiple_of(p * half + which * (half - shared), 16), shared)

    def y_copy(p, sign, t, which):
        where = params_out.at[y_rows(p, which), place(-sign * (t + 1))]
        i = y_number(sign, t)
        return pltpu.make_async_remote_copy(
            src_ref=where, dst_ref=where,
            send_sem=y_send.at[p, i], recv_sem=y_recv.at[p, i],
            device_id={"group": partner}, device_id_type=MESH)

    def fy_copy(p, sign, t, c):
        where = params_out.at[y_rows(p, 1 - parity), columns(2 * chip_at(-sign * (t + 1)) + c)]
        i = y_number(sign, t)
        return pltpu.make_async_remote_copy(
            src_ref=where, dst_ref=where,
            send_sem=fy_send.at[p, i], recv_sem=fy_recv.at[p, i],
            device_id={"shard": sibling}, device_id_type=MESH)

    trips = [(t, first) for t in range(steps) for first in ((True, False) if t < steps - 1 else (True,))]
    number = {trip: m for m, trip in enumerate(trips)}

    def own_copy(p):
        here = pl.ds(p * half, half)
        return pltpu.make_async_copy(param.at[here, :], params_out.at[here, place(0)], own_sem.at[p])

    def own_forward(p, c):
        here = pl.ds(p * half, half)
        return pltpu.make_async_remote_copy(
            src_ref=param.at[here, :], dst_ref=params_out.at[here, columns(2 * chip + c)],
            send_sem=fw_send.at[2 * p, count], recv_sem=fw_recv.at[2 * p, count],
            device_id={"shard": sibling}, device_id_type=MESH)

    sent = []
    pending = []
    y_done = []

    def go(p, sign, t, first):
        if (t, first) in number:
            copy = ag_copy(p, sign, t, first)
            copy.start()
            sent.append(copy)

    def gather_start(p):
        for first in (True, False):
            for sign in (1, -1):
                go(p, sign, 0, first)
        own_copy(p).start()
        own_forward(p, core).start()

    def y_take():
        p, sign, t = pending.pop(0)
        y_copy(p, sign, t, 1 - parity).wait_recv()
        fy_copy(p, sign, t, core).start()
        y_done.append((p, sign, t))

    def y_give(p, sign, t):
        if paired:
            y_copy(p, sign, t, parity).start()
            pending.append((p, sign, t))

    def gather_event(p, t, first):
        for sign in (1, -1):
            ag_arrival(p, sign, t, first).wait_recv()
            go(p, sign, t + 1, first)
            fw_copy(p, sign, t, first, core).start()
            if not first:
                y_give(p, sign, t)
        if t == steps - 1:
            y_give(p, 1, t)
        while len(pending) > 3:
            y_take()

    waves = [(0, True)]
    for t in range(1, steps):
        waves += [(t, False), (t, True)]
    sum_step(0, *waves[0])
    sum_step(0, *waves[1])
    for copy in operands:
        copy.wait()
    lay_indices(0)
    for wave in waves[2:]:
        sum_step(0, *wave)
    for wave in waves[:2]:
        sum_step(1, *wave)
    sum_end(0)
    forward(0)
    for wave in waves[2:-2]:
        sum_step(1, *wave)
    for k in range(1, n_group):
        idx_copies[k - 1].wait_recv()
        lay_indices(k)
    update(0)
    for wave in waves[-2:]:
        sum_step(1, *wave)
    gather_start(0)
    sum_end(1)
    forward(1)
    for trip in trips[:2]:
        gather_event(0, *trip)
    update(1)
    gather_start(1)
    momentum_half(0)
    left = trips[2:]
    others = list(trips)
    turn = 0
    while left or others:
        for trip in left[:2]:
            gather_event(0, *trip)
        left = left[2:]
        for trip in others[:2]:
            gather_event(1, *trip)
        others = others[2:]
        if turn == 0:
            momentum_half(1)
        turn += 1
    while pending:
        y_take()

    for p in range(2):
        for t, first in trips:
            for sign in (1, -1):
                fw_copy(p, sign, t, first, core).wait_send()
                fw_copy(p, sign, t, first, 1 - core).wait_recv()
        own_forward(p, core).wait_send()
        own_forward(p, 1 - core).wait_recv()
        own_copy(p).wait()
    for p, sign, t in y_done:
        y_copy(p, sign, t, parity).wait_send()
        fy_copy(p, sign, t, core).wait_send()
        fy_copy(p, sign, t, 1 - core).wait_recv()
    for copy in sent:
        copy.wait_send()
    for r in order:
        raw[r].wait_send()
    for p in range(2):
        for sign in (1, -1):
            for m in range(count):
                for copy in q_copies(p, sign, m):
                    copy.wait_send()
        for k in range(1, n_group):
            pick_copy(p, k).wait_send()
    for copy in idx_copies:
        copy.wait_send()


def local(n_group, n_shard, gradients, momentum, master, indices):
    rows, width = master.shape
    whole = gradients.shape[3]
    n = n_shard // 2
    steps = n // 2
    count = 2 * steps - 1
    height = rows // BLOCK
    slots = indices.shape[2] * indices.shape[3]
    idx = indices.reshape(-1, indices.shape[3])
    span = 256 if width % 256 == 0 else 128
    table = cosine_table(BLOCK)
    rt = np.kron(np.eye(height // 2), table).astype(np.float32)
    ct = np.kron(np.eye(span // BLOCK), table).astype(np.float32)
    others = max(n_group - 1, 1)
    dma = pltpu.SemaphoreType.DMA
    vmem = pl.BlockSpec(memory_space=pltpu.VMEM)
    hbm = pl.BlockSpec(memory_space=pltpu.HBM)
    free = pl.BlockSpec(memory_space=pl.ANY)
    body = functools.partial(kernel, n_group, n, width)
    return pl.pallas_call(
        body,
        out_shape=(
            jax.ShapeDtypeStruct((1, rows, width), F32),
            jax.ShapeDtypeStruct((rows, width), F32),
            jax.ShapeDtypeStruct((rows, whole), BF16),
        ),
        in_specs=[hbm] * 7,
        out_specs=(vmem, vmem, free),
        scratch_shapes=[
            pltpu.VMEM((n, rows, width), BF16),
            pltpu.VMEM((n, rows, width), BF16),
            pltpu.VMEM((4, count, rows // 4, width), jnp.int16),
            pltpu.VMEM((4, count, rows // 4, width), jnp.int16),
            pltpu.VMEM((4, count, 8, LANES), F32),
            pltpu.VMEM((4, count, 8, LANES), F32),
            pltpu.VMEM((rows, width), F32),
            pltpu.VMEM((rows, width), F32),
            pltpu.VMEM((rows, width), BF16),
            pltpu.VMEM((n_group,) + idx.shape, jnp.int32),
            pltpu.VMEM((n_group, -(-height // 8) * 8, slots), jnp.int32),
            pltpu.VMEM((n_group, 2, 8, slots), F32),
            pltpu.VMEM((rows, width), F32),
            pltpu.VMEM((rows, width), F32),
            pltpu.VMEM(rt.shape, F32),
            pltpu.VMEM(rt.shape, F32),
            pltpu.VMEM(ct.shape, F32),
            dma((n,)), dma((n,)), dma((n,)),
            dma((4, count)), dma((4, count)), dma((4, count)), dma((4, count)),
            dma((others,)), dma((others,)), dma((2, others)), dma((2, others)), dma((6,)),
            dma((2,)), dma((4, count)), dma((4, count)), dma((4, count + 1)), dma((4, count + 1)),
            dma((2, count)), dma((2, count)), dma((2, count)), dma((2, count)),
        ],
        compiler_params=pltpu.CompilerParams(
            collective_id=0, has_side_effects=True, vmem_limit_bytes=58 * 1024 * 1024),
        cost_estimate=pl.CostEstimate(
            flops=30 * rows * rows * width, bytes_accessed=4 * rows * whole, transcendentals=rows * width),
    )(gradients, momentum, master, idx, jnp.asarray(rt), jnp.asarray(rt.T.copy()), jnp.asarray(ct))


def solution(mesh):
    placed = (
        P("group", "shard", None, None),
        P("group", None, "shard"),
        P(None, "shard"),
        P("group", None, "shard", None),
    )
    return jax.shard_map(
        functools.partial(local, mesh.shape["group"], mesh.shape["shard"]),
        mesh=mesh,
        in_specs=placed,
        out_specs=(P("group", None, "shard"), P(None, "shard"), P()),
        check_vma=False,
    )
```
